256 devices in a mesh: row: 32 (over z, x), col: 8 (over y, core).
Axes of the slice: x: 4, y: 4, z: 8, core: 2. Of those that a mesh axis runs over, the one named last changes fastest.
Arguments:
- node_features: bfloat16 [65536, 768], P(('row', 'col')), may hold values from -6 to 6
- neighbour_count: int32 [65536], P(('row', 'col')), may hold values from 1 to 64
- tile_rows: int32 [32, 8, 128], P('row', 'col'), may hold values from 0 to 15
- tile_cols: int32 [32, 8, 128], P('row', 'col'), may hold values from 0 to 63
- tile_count: int32 [32, 8], P('row', 'col'), may hold values from 32 to 128, as said below
- patterns: int32 [32, 8, 128, 128, 128], P('row', 'col'), may hold values 0 or 1
- w_self: float32 [768, 256], replicated, may hold values from -0.21875 to 0.21875
- w_neigh: float32 [768, 256], replicated, may hold values from -0.21875 to 0.21875
- bias: float32 [256], replicated, may hold values from -3 to 3
Outputs:
- out: float32 [65536, 256], P(('row', 'col'))
The draws below stay inside these ranges and needn't reach their ends.
Inputs may be any that keep to these rules, and one draw needn't show every extreme that they name: `tile_count`: number of slots of a cell that are used; slots at or beyond it are ignored.
All inputs are finite; a program needn't handle non-finite values. No bound on the sum of `patterns` on one device may be relied on, other than what follows from the above.
Results may differ from the reference program's by a relative error of at most 0.0003.
Values may be sent and summed in bfloat16 or wider, within the bound.
No kernel may reach another device: no remote copies, remote signals or barrier semaphores. Data moves between devices by JAX's collectives and lax.ppermute only.
A program may use at most 128 MiB of HBM per device.

```python
import jax
import jax.numpy as jnp
from jax import lax

F = 768
H = 256
TILE = 128
CH = 256
TMAX = 128
NODES = 65536
N_ROW = 32
N_COL = 8


def draw_tile_count(key, part):
    key = jax.random.fold_in(key, 7)
    first_key = jax.random.fold_in(key, 1)
    second_key = jax.random.fold_in(key, 2)
    cell_total = N_ROW * N_COL
    counts = jax.random.randint(first_key, (cell_total,), TMAX // 4, TMAX + 1)
    full_cell = jax.random.randint(second_key, (), 0, cell_total)
    position = jnp.arange(cell_total)
    counts = jnp.where(position == full_cell, TMAX, counts)
    counts = jnp.where(position == (full_cell + 1) % cell_total, TMAX // 4, counts)
    return counts.reshape(N_ROW, N_COL).astype(jnp.int32)


def touch_ends(drawn, key, least, high):
    longest = drawn.shape.index(max(drawn.shape))
    spots = []
    for shift in (0, 1):
        where = [jax.random.randint(jax.random.fold_in(key, axis), (), 0, length) for axis, length in enumerate(drawn.shape)]
        where[longest] = (where[longest] + shift) % drawn.shape[longest]
        spots.append(tuple(where))
    return drawn.at[spots[0]].set(least).at[spots[1]].set(high)


def steps_of(stream_key, dims, cuts, smallest, largest):
    factor_of, own = 1.0, jax.random.fold_in(stream_key, 6)
    for dim, parts in cuts:
        steps = jnp.exp(jax.random.uniform(jax.random.fold_in(own, dim), (parts,), jnp.float32, smallest / len(cuts), largest / len(cuts)))
        factor_of = factor_of * jnp.repeat(steps, dims[dim] // parts).reshape([-1 if axis == dim else 1 for axis in range(len(dims))])
    return factor_of


def gaussian(key, extent, spread, bound, split=(), kind=jnp.bfloat16):
    array = jax.random.normal(key, extent, jnp.float32) * spread
    if len(split) > 0:
        array = steps_of(key, extent, split, -0.22, 0.18) * array
    return jnp.clip(array, min=-bound, max=bound).astype(kind)


def setup_inputs(seed: int = 0) -> dict:
    key_of = jax.random.split(jax.random.key(seed), 10)
    node_features = gaussian(key_of[0], (NODES, F), 1.0, 6.0, ((0, 256),))
    neighbour_count = touch_ends(jax.random.randint(key_of[1], (NODES,), 1, 65), jax.random.fold_in(key_of[1], 1), 1, 64).astype(jnp.int32)
    tile_rows = touch_ends(jax.random.randint(key_of[2], (N_ROW, N_COL, TMAX), 0, N_COL * CH // TILE), jax.random.fold_in(key_of[2], 1), 0, (N_COL * CH // TILE) - 1).astype(jnp.int32)
    tile_cols = touch_ends(jax.random.randint(key_of[3], (N_ROW, N_COL, TMAX), 0, N_ROW * CH // TILE), jax.random.fold_in(key_of[3], 1), 0, (N_ROW * CH // TILE) - 1).astype(jnp.int32)
    tile_count = draw_tile_count(jax.random.fold_in(key_of[9], 71), 0)
    patterns = touch_ends((jax.random.randint(key_of[5], (N_ROW, N_COL, TMAX, TILE, TILE), 0, 16) < 1).astype(jnp.int32), jax.random.fold_in(key_of[5], 1), 0, 1)
    w_self = gaussian(key_of[6], (F, H), F ** -0.5, 0.21875, (), jnp.float32)
    w_neigh = gaussian(key_of[7], (F, H), F ** -0.5, 0.21875, (), jnp.float32)
    bias = gaussian(key_of[8], (H,), 0.5, 3.0, (), jnp.float32)
    return dict(node_features=node_features, neighbour_count=neighbour_count, tile_rows=tile_rows, tile_cols=tile_cols, tile_count=tile_count, patterns=patterns, w_self=w_self, w_neigh=w_neigh, bias=bias)


def reference(node_features, neighbour_count, tile_rows, tile_cols, tile_count, patterns, w_self, w_neigh, bias):
    precise = lax.Precision.HIGHEST
    features = node_features.astype(jnp.float32)
    row_tiles = N_COL * CH // TILE
    blocks = features.reshape(N_ROW, N_COL, CH, F)
    columns = jnp.transpose(blocks, (1, 0, 2, 3)).reshape(N_COL, N_ROW * CH // TILE, TILE, F)
    slot_index = jnp.arange(TMAX, dtype=jnp.int32)

    def one_cell(row_index, col_index):
        picked = jnp.take(columns[col_index], tile_cols[row_index, col_index], axis=0)
        live_slot = slot_index < tile_count[row_index, col_index]
        pattern_block = jnp.where(live_slot[:, None, None], patterns[row_index, col_index], 0).astype(jnp.float32)
        product = jnp.einsum("sij,sjf->sif", pattern_block, picked, precision=precise)
        empty = jnp.zeros((row_tiles, TILE, F), jnp.float32)
        return empty.at[tile_rows[row_index, col_index]].add(product)

    def one_row(row_index):
        def add_cell(col_index, running):
            return running + one_cell(row_index, col_index)
        return lax.fori_loop(0, N_COL, add_cell, jnp.zeros((row_tiles, TILE, F), jnp.float32))

    summed = lax.map(one_row, jnp.arange(N_ROW, dtype=jnp.int32)).reshape(N_ROW * N_COL * CH, F)
    mean_rows = summed / neighbour_count.astype(jnp.float32)[:, None]
    own_part = jnp.dot(features, w_self, precision=precise)
    neighbour_part = jnp.dot(mean_rows, w_neigh, precision=precise)
    return jax.nn.relu(own_part + neighbour_part + bias)
```

```python
import functools

import jax
import jax.numpy as jnp
from jax import lax
from jax.experimental import pallas as pl
from jax.experimental.pallas import tpu as pltpu
from jax.sharding import PartitionSpec as P

Z, X, Y, CORES = 8, 4, 4, 2
SPAN = 256
TILE = 128
H = 256
LANES = 128
WORDS = H // 2
SHARD = SPAN + 8
Z_ORDER = (0, 1, 4, 7, 2, 5, 6, 3)
Z_PLACE = tuple(Z_ORDER.index(d) for d in range(Z))
VMEM_LIMIT = 56 * 1024 * 1024
BF, F32, I32 = jnp.bfloat16, jnp.float32, jnp.int32


def encode(values, out_ref):
    size = jnp.maximum(jnp.max(jnp.abs(values), axis=1, keepdims=True), 2.0**-100)
    exponent = jnp.zeros(size.shape, I32)
    factor = jnp.full(size.shape, 2.0**14, F32)
    for k in (32, 16, 8, 4, 2, 1):
        big = size >= 2.0**k
        size = jnp.where(big, size * 2.0**-k, size)
        factor = jnp.where(big, factor * 2.0**-k, factor)
        exponent = jnp.where(big, exponent + k, exponent)
    for k in (64, 32, 16, 8, 4, 2, 1):
        small = size < 2.0 ** (1 - k)
        size = jnp.where(small, size * 2.0**k, size)
        factor = jnp.where(small, factor * 2.0**k, factor)
        exponent = jnp.where(small, exponent - k, exponent)
    codes = jnp.clip(jnp.floor(values * factor + 0.5), -32767.0, 32767.0).astype(I32)
    out_ref[:SPAN, :] = (codes[:, :WORDS] << 16) | (codes[:, WORDS:] & 0xFFFF)
    along = jnp.transpose(jnp.broadcast_to(exponent, (SPAN, LANES)))
    out_ref[SPAN : SPAN + 8, :] = jnp.zeros((8, LANES), I32)
    for half in range(SPAN // LANES):
        out_ref[SPAN + half : SPAN + half + 1, :] = along[:1, half * LANES : (half + 1) * LANES]


def power_of_two(exponent):
    left = exponent + (120 - 14)
    result = jnp.full(exponent.shape, 2.0**-120, F32)
    for bit in range(7):
        result = jnp.where((left >> bit) & 1 == 1, result * 2.0 ** (1 << bit), result)
    return jnp.where((left >> 7) & 1 == 1, result * 2.0**64 * 2.0**64, result)


def two_codes(words):
    return (words >> 16).astype(F32), ((words << 16) >> 16).astype(F32)


def project_kernel(x_ref, w_ref, out_ref):
    w = w_ref[...]
    high = w.astype(BF)
    low = (w - high.astype(F32)).astype(BF)
    x = x_ref[...]
    z = jnp.dot(x, high, preferred_element_type=F32) + jnp.dot(x, low, preferred_element_type=F32)
    encode(z, out_ref)


def project(x, w):
    return pl.pallas_call(
        project_kernel,
        out_shape=jax.ShapeDtypeStruct((SHARD, WORDS), I32),
        compiler_params=pltpu.CompilerParams(vmem_limit_bytes=VMEM_LIMIT),
        name="project",
    )(x, w)


def aggregate_kernel(layout, slots_ref, pat_hbm, *refs):
    pieces = refs[: len(layout)]
    keep_ref, send_ref, raw, parts, scales, pat, acc, piece_sem, pat_sem = refs[len(layout) :]
    slot_total = pat_hbm.shape[0]
    copies = []
    for n, (first, count) in enumerate(layout):
        copy = pltpu.make_async_copy(
            pieces[n], raw.at[pl.ds(first * SHARD, count * SHARD)], piece_sem.at[n]
        )
        copy.start()
        copies.append(copy)
    pat_copy = pltpu.make_async_copy(pat_hbm, pat, pat_sem)
    pat_copy.start()
    acc[...] = jnp.zeros_like(acc)

    def decode(shard, carry):
        base = pl.multiple_of(shard * SHARD, 8)
        exponents = raw[pl.ds(base + SPAN, 8), :]
        scale = power_of_two(exponents)
        for half in range(2):
            words = raw[pl.ds(base + half * TILE, TILE), :]
            tile = shard * 2 + half
            scales[tile] = jnp.broadcast_to(scale[half : half + 1], (8, LANES))
            for side, code in enumerate(two_codes(words)):
                high = code.astype(BF)
                low = (code - high.astype(F32)).astype(BF)
                at = pl.ds(side * WORDS, WORDS)
                parts[tile, :TILE, at] = high
                parts[tile, TILE:, at] = low
        return carry

    for n, (first, count) in enumerate(layout):
        copies[n].wait()
        lax.fori_loop(first, first + count, decode, 0)
    pat_copy.wait()
    live = slots_ref[2, 0]
    group = 4

    def add_group(g, carry):
        for k in range(group):
            s = g * group + k
            row, col = slots_ref[0, s], slots_ref[1, s]
            scale = jnp.where(s < live, scales[col], 0.0)[:1].astype(BF)
            p = pat[s] * scale
            acc[row] += jnp.dot(
                jnp.concatenate([p, p], axis=1), parts[col], preferred_element_type=F32
            )
        return carry

    lax.fori_loop(0, (live + group - 1) // group, add_group, 0)
    half = acc.shape[0] // 2
    keep_ref[...] = acc[:half].reshape(keep_ref.shape)
    send_ref[...] = acc[half:].reshape(send_ref.shape)


def aggregate(slots, pat, pieces, layout, row_tiles):
    half_rows = row_tiles * TILE // 2
    shards = sum(count for _, count in layout)
    return pl.pallas_call(
        functools.partial(aggregate_kernel, layout),
        out_shape=[jax.ShapeDtypeStruct((half_rows, H), F32)] * 2,
        in_specs=[pl.BlockSpec(memory_space=pltpu.SMEM)]
        + [pl.BlockSpec(memory_space=pl.ANY)] * (1 + len(pieces)),
        out_specs=[pl.BlockSpec(memory_space=pltpu.VMEM)] * 2,
        scratch_shapes=[
            pltpu.VMEM((shards * SHARD, WORDS), I32),
            pltpu.VMEM((shards * 2, 2 * TILE, H), BF),
            pltpu.VMEM((shards * 2, 8, LANES), F32),
            pltpu.VMEM(pat.shape, BF),
            pltpu.VMEM((row_tiles, TILE, H), F32),
            pltpu.SemaphoreType.DMA((len(pieces),)),
            pltpu.SemaphoreType.DMA,
        ],
        compiler_params=pltpu.CompilerParams(vmem_limit_bytes=VMEM_LIMIT),
        name="aggregate",
    )(slots, pat, *pieces)


def pair_kernel(keep_ref, other_ref, own_ref, *pay_refs):
    own_ref[...] = keep_ref[:SPAN] + other_ref[:SPAN]
    for j, pay_ref in enumerate(pay_refs, 1):
        at = pl.ds(j * SPAN, SPAN)
        encode(keep_ref[at] + other_ref[at], pay_ref)


def add_pair(keep, other):
    return pl.pallas_call(
        pair_kernel,
        out_shape=[jax.ShapeDtypeStruct((SPAN, H), F32)]
        + [jax.ShapeDtypeStruct((SHARD, WORDS), I32)] * (Y - 1),
        compiler_params=pltpu.CompilerParams(vmem_limit_bytes=VMEM_LIMIT),
        name="add_pair",
    )(keep, other)


def self_kernel(x_ref, w_ref, bias_ref, out_ref):
    w = w_ref[...]
    high = w.astype(BF)
    low = (w - high.astype(F32)).astype(BF)
    x = x_ref[...]
    z = jnp.dot(x, high, preferred_element_type=F32) + jnp.dot(x, low, preferred_element_type=F32)
    out_ref[...] = z + bias_ref[...]


def self_part(x, w, bias):
    return pl.pallas_call(
        self_kernel,
        out_shape=jax.ShapeDtypeStruct((SPAN, H), F32),
        compiler_params=pltpu.CompilerParams(vmem_limit_bytes=VMEM_LIMIT),
        name="self_part",
    )(x, w, bias)


def finish_kernel(own_ref, self_ref, count_ref, *refs):
    out_ref = refs[-1]
    divisor = count_ref[...].astype(F32)
    for half in range(SPAN // TILE):
        at = pl.ds(half * TILE, TILE)
        left, right = own_ref[at, :WORDS], own_ref[at, WORDS:]
        for pay_ref in refs[:-1]:
            row = pay_ref[SPAN + half : SPAN + half + 1, :]
            scale = jnp.transpose(jnp.broadcast_to(power_of_two(row), (TILE, LANES)))
            a, b = two_codes(pay_ref[at, :])
            left, right = left + a * scale, right + b * scale
        d = divisor[half * TILE : (half + 1) * TILE]
        out_ref[at, :WORDS] = jnp.maximum(left / d + self_ref[at, :WORDS], 0.0)
        out_ref[at, WORDS:] = jnp.maximum(right / d + self_ref[at, WORDS:], 0.0)


def finish(own, self_rows, count, pays):
    return pl.pallas_call(
        finish_kernel,
        out_shape=jax.ShapeDtypeStruct((SPAN, H), F32),
        compiler_params=pltpu.CompilerParams(vmem_limit_bytes=VMEM_LIMIT),
        name="finish",
    )(own, self_rows, count, *pays)


def from_z(x, d):
    return lax.ppermute(x, "row", [(((z + d) % Z) * X + k, z * X + k) for z in range(Z) for k in range(X)])


def from_x(x, d):
    return lax.ppermute(x, "row", [(z * X + (k + d) % X, z * X + k) for z in range(Z) for k in range(X)])


def from_y(x, d):
    return lax.ppermute(
        x, "col", [(((y + d) % Y) * CORES + k, y * CORES + k) for y in range(Y) for k in range(CORES)]
    )


def from_core(x):
    return lax.ppermute(x, "col", [(c ^ 1, c) for c in range(Y * CORES)])


def z_near(block):
    near, far, last = from_z(block, 1), from_z(block, 4), from_z(block, -1)
    return jnp.concatenate([near, far, last])


def z_rest(near):
    up = from_z(near[: 2 * SHARD], 1)
    down = from_z(jnp.concatenate([near[2 * SHARD :], near[SHARD : 2 * SHARD]]), -1)
    return up, down


def body(
    node_features, neighbour_count, tile_rows, tile_cols, tile_count, patterns, w_self, w_neigh, bias
):
    row_tiles = Y * CORES * SPAN // TILE
    mine = project(node_features, w_neigh)

    across = from_x(mine, 2)
    side_0 = [from_x(mine, 1), from_x(mine, -1)]
    near = z_near(mine)
    across_near = z_near(across)
    side_1 = [from_x(near, 1), from_x(near, -1)]
    up, down = z_rest(near)
    across_up, across_down = z_rest(across_near)
    rest = jnp.concatenate([up, down])
    side_2 = [from_x(rest, 1), from_x(rest, -1)]

    row_at, col_at = lax.axis_index("row"), lax.axis_index("col")
    z_at, x_at = row_at // X, row_at % X
    y_at, core_at = col_at // CORES, col_at % CORES
    cols = tile_cols[0, 0]
    source = cols // 2
    dz = (source // X - z_at) % Z
    dx = (source % X - x_at) % X
    place = jnp.take(jnp.asarray(Z_PLACE, I32), dz)
    col_index = (dx * Z + place) * 2 + cols % 2
    rows = tile_rows[0, 0]
    span = rows // 2
    other = (span % CORES != core_at).astype(I32)
    row_index = other * (row_tiles // 2) + ((span // CORES - y_at) % Y) * 2 + rows % 2
    slots = jnp.stack([row_index, col_index, jnp.broadcast_to(tile_count[0, 0], rows.shape)])

    pieces = [mine, near, rest, side_0[0], side_1[0], side_2[0], across, across_near, across_up, across_down,
              side_0[1], side_1[1], side_2[1]]
    layout = [(0, 1), (1, 3), (4, 4), (8, 1), (9, 3), (12, 4), (16, 1), (17, 3), (20, 2), (22, 2),
              (24, 1), (25, 3), (28, 4)]
    keep, send = aggregate(slots, patterns[0, 0].astype(BF), pieces, layout, row_tiles)

    own, *pays = add_pair(keep, from_core(send))
    pays = [from_y(pay, -j) for j, pay in enumerate(pays, 1)]
    self_rows = self_part(node_features, w_self, bias[None, :])
    return finish(own, self_rows, neighbour_count[:, None], pays)


def solution(mesh):
    return jax.shard_map(
        body,
        mesh=mesh,
        in_specs=(
            P(("row", "col"), None),
            P(("row", "col")),
            P("row", "col", None),
            P("row", "col", None),
            P("row", "col"),
            P("row", "col", None, None, None),
            P(),
            P(),
            P(),
        ),
        out_specs=P(("row", "col"), None),
        check_vma=False,
    )
```

```python
import functools

import jax
import jax.numpy as jnp
from jax import lax
from jax.experimental import pallas as pl
from jax.experimental.pallas import tpu as pltpu
from jax.sharding import PartitionSpec as P

Z, X, Y, CORES = 8, 4, 4, 2
SPAN = 256
TILE = 128
H = 256
LANES = 128
WORDS = H // 2
SHARD = SPAN + 8
GROUP = 16
EARLY = 20
STEPS = (0, 1, -1, 2)
VMEM_LIMIT = 20 * 1024 * 1024
BF, F32, I32 = jnp.bfloat16, jnp.float32, jnp.int32


def encode(values, out_ref):
    size = jnp.maximum(jnp.max(jnp.abs(values), axis=1, keepdims=True), 2.0**-100)
    exponent = jnp.floor(jnp.log2(size) + 0.001)
    codes = jnp.floor(values * jnp.exp2(14.0 - exponent) + 0.5).astype(I32)
    out_ref[:SPAN, :] = (codes[:, :WORDS] << 16) | (codes[:, WORDS:] & 0xFFFF)
    along = jnp.transpose(jnp.broadcast_to(exponent, (SPAN, LANES))).astype(I32)
    out_ref[SPAN : SPAN + 8, :] = jnp.zeros((8, LANES), I32)
    for half in range(SPAN // LANES):
        out_ref[SPAN + half : SPAN + half + 1, :] = along[:1, half * LANES : (half + 1) * LANES]


def power_of_two(exponent):
    left = exponent + (120 - 14)
    result = jnp.full(exponent.shape, 2.0**-120, F32)
    for bit in range(7):
        result = jnp.where((left >> bit) & 1 == 1, result * 2.0 ** (1 << bit), result)
    return jnp.where((left >> 7) & 1 == 1, result * 2.0**64 * 2.0**64, result)


def two_codes(words):
    return (words >> 16).astype(F32), ((words << 16) >> 16).astype(F32)


def vmem(*arrays):
    return [pltpu.with_memory_space_constraint(array, pltpu.VMEM) for array in arrays]


IN_VMEM = pl.BlockSpec(memory_space=pltpu.VMEM)


def project_kernel(x_ref, w_ref, out_ref):
    w = w_ref[...]
    high = w.astype(BF)
    low = (w - high.astype(F32)).astype(BF)
    x = x_ref[...]
    z = jnp.dot(x, high, preferred_element_type=F32) + jnp.dot(x, low, preferred_element_type=F32)
    encode(z, out_ref)


def project(x, w):
    return pl.pallas_call(
        project_kernel,
        out_shape=pltpu.VMEM((SHARD, WORDS), I32),
        compiler_params=pltpu.CompilerParams(vmem_limit_bytes=VMEM_LIMIT),
        name="project",
    )(x, w)


def load_kernel(pat_hbm, after_ref, out_ref, zero_ref, landing, sem):
    chunk, depth = landing.shape[1], landing.shape[0]
    steps = pat_hbm.shape[0] // chunk

    def fetch(step):
        slot = step % depth
        return pltpu.make_async_copy(pat_hbm.at[pl.ds(step * chunk, chunk)], landing.at[slot], sem.at[slot])

    for step in range(depth):
        fetch(step).start()
    for step in range(steps):
        fetch(step).wait()
        out_ref[step * chunk : (step + 1) * chunk] = landing[step % depth].astype(BF)
        if step + depth < steps:
            fetch(step + depth).start()
    zero_ref[...] = after_ref[SPAN + 2 : SPAN + 3, :1]


def load_patterns(patterns, after):
    return pl.pallas_call(
        load_kernel,
        out_shape=[pltpu.VMEM(patterns.shape, BF), jax.ShapeDtypeStruct((1, 1), I32)],
        in_specs=[pl.BlockSpec(memory_space=pltpu.HBM), IN_VMEM],
        out_specs=[IN_VMEM, IN_VMEM],
        scratch_shapes=[pltpu.VMEM((4, 8, TILE, TILE), I32), pltpu.SemaphoreType.DMA((4,))],
        compiler_params=pltpu.CompilerParams(vmem_limit_bytes=VMEM_LIMIT),
        name="load_patterns",
    )(pltpu.with_memory_space_constraint(patterns, pltpu.HBM), *vmem(after))


def aggregate_kernel(late, counts, slots_ref, pat, *refs):
    pieces, refs = refs[: len(counts)], refs[len(counts) :]
    if late:
        first_ref, keep_ref, send_ref, parts, scales, acc = refs
    else:
        acc, parts, scales = refs
    start = slots_ref[3, 0] if late else 0
    stop = slots_ref[4, 0] if late else slots_ref[3, 0]
    groups = (stop - start + GROUP - 1) // GROUP

    acc[...] = first_ref[...] if late else jnp.zeros_like(acc)

    at = 0
    for piece, count in zip(pieces, counts):

        def decode(n, carry, piece=piece, at=at):
            base = pl.multiple_of(n * SHARD, 8)
            scale = power_of_two(piece[pl.ds(base + SPAN, 8), :])
            for half in range(2):
                words = piece[pl.ds(base + half * TILE, TILE), :]
                tile = (at + n) * 2 + half
                scales[tile] = jnp.broadcast_to(scale[half : half + 1], (8, LANES))
                for side, code in enumerate(two_codes(words)):
                    high = code.astype(BF)
                    low = (code - high.astype(F32)).astype(BF)
                    where = pl.ds(side * WORDS, WORDS)
                    parts[tile, :TILE, where] = high
                    parts[tile, TILE:, where] = low
            return carry

        lax.fori_loop(0, count, decode, 0)
        at += count

    def add_group(g, carry):
        for k in range(GROUP):
            n = start + g * GROUP + k
            at = jnp.minimum(n, pat.shape[0] - 1)
            row, col = slots_ref[0, at], jnp.where(n < stop, slots_ref[1, at], 0)
            p = pat[slots_ref[2, at]] * jnp.where(n < stop, scales[col], 0.0)[:1].astype(BF)
            acc[row] += jnp.dot(
                jnp.concatenate([p, p], axis=1), parts[col], preferred_element_type=F32
            )
        return carry

    lax.fori_loop(0, groups, add_group, 0)
    if late:
        keep_ref[...] = acc[: acc.shape[0] // 2]
        send_ref[...] = acc[acc.shape[0] // 2 :]


def aggregate(slots, pat, pieces, row_tiles, first=None):
    late = first is not None
    counts = tuple(piece.shape[0] // SHARD for piece in pieces)
    shards = sum(counts)
    sums = pltpu.VMEM((row_tiles, TILE, H), F32)
    half = pltpu.VMEM((row_tiles // 2, TILE, H), F32)
    operands = vmem(pat, *pieces, first) if late else vmem(pat, *pieces)
    return pl.pallas_call(
        functools.partial(aggregate_kernel, late, counts),
        out_shape=[half, half] if late else sums,
        in_specs=[pl.BlockSpec(memory_space=pltpu.SMEM)] + [IN_VMEM] * len(operands),
        out_specs=[IN_VMEM, IN_VMEM] if late else IN_VMEM,
        scratch_shapes=[
            pltpu.VMEM((shards * 2, 2 * TILE, H), BF),
            pltpu.VMEM((shards * 2, 8, LANES), F32),
        ]
        + [sums] * late,
        compiler_params=pltpu.CompilerParams(vmem_limit_bytes=VMEM_LIMIT),
        name="aggregate_late" if late else "aggregate_early",
    )(slots, *operands)


def pair_kernel(keep_ref, other_ref, own_ref, *pay_refs):
    tiles = SPAN // TILE
    for j in range(Y):
        at = pl.ds(j * tiles, tiles)
        both = (keep_ref[at] + other_ref[at]).reshape(SPAN, H)
        if j == 0:
            own_ref[...] = both
        else:
            encode(both, pay_refs[j - 1])


def add_pair(keep, other):
    return pl.pallas_call(
        pair_kernel,
        out_shape=[pltpu.VMEM((SPAN, H), F32)] + [pltpu.VMEM((SHARD, WORDS), I32)] * (Y - 1),
        in_specs=[IN_VMEM] * 2,
        out_specs=[IN_VMEM] * Y,
        compiler_params=pltpu.CompilerParams(vmem_limit_bytes=VMEM_LIMIT),
        name="add_pair",
    )(*vmem(keep, other))


def self_kernel(x_ref, w_ref, bias_ref, out_ref):
    w = w_ref[...]
    high = w.astype(BF)
    low = (w - high.astype(F32)).astype(BF)
    x = x_ref[...]
    z = jnp.dot(x, high, preferred_element_type=F32) + jnp.dot(x, low, preferred_element_type=F32)
    out_ref[...] = z + bias_ref[...]


def self_part(x, w, bias):
    return pl.pallas_call(
        self_kernel,
        out_shape=pltpu.VMEM((SPAN, H), F32),
        out_specs=IN_VMEM,
        compiler_params=pltpu.CompilerParams(vmem_limit_bytes=VMEM_LIMIT),
        name="self_part",
    )(x, w, bias)


def finish_kernel(own_ref, self_ref, count_ref, *refs):
    out_ref = refs[-1]
    for half in range(SPAN // TILE):
        at = pl.ds(half * TILE, TILE)
        left, right = own_ref[at, :WORDS], own_ref[at, WORDS:]
        for pay_ref in refs[:-1]:
            row = pay_ref[SPAN + half : SPAN + half + 1, :]
            scale = jnp.transpose(jnp.broadcast_to(power_of_two(row), (TILE, LANES)))
            a, b = two_codes(pay_ref[at, :])
            left, right = left + a * scale, right + b * scale
        d = jnp.transpose(jnp.broadcast_to(count_ref[half : half + 1].astype(F32), (TILE, LANES)))
        out_ref[at, :WORDS] = jnp.maximum(left / d + self_ref[at, :WORDS], 0.0)
        out_ref[at, WORDS:] = jnp.maximum(right / d + self_ref[at, WORDS:], 0.0)


def finish(own, self_rows, count, pays):
    return pl.pallas_call(
        finish_kernel,
        out_shape=jax.ShapeDtypeStruct((SPAN, H), F32),
        compiler_params=pltpu.CompilerParams(vmem_limit_bytes=VMEM_LIMIT),
        in_specs=[IN_VMEM] * (3 + len(pays)),
        name="finish",
    )(*vmem(own, self_rows), count, *vmem(*pays))


def from_far_z(x):
    return lax.ppermute(x, "row", [(((z + Z // 2) % Z) * X + k, z * X + k) for z in range(Z) for k in range(X)])


def from_step(x, step, x_core):
    pairs = []
    for z in range(Z):
        for k in range(X):
            for c in range(Y * CORES):
                if c % CORES == x_core:
                    source = z * X + (k + step) % X
                else:
                    source = ((z + (-step if step == 2 and z % 2 else step)) % Z) * X + k
                pairs.append((source * Y * CORES + c, (z * X + k) * Y * CORES + c))
    return lax.ppermute(x, ("row", "col"), pairs)


def from_y(x, d):
    return lax.ppermute(
        x, "col", [(((y + d) % Y) * CORES + k, y * CORES + k) for y in range(Y) for k in range(CORES)]
    )


def from_core(x):
    return lax.ppermute(x, "col", [(c ^ 1, c) for c in range(Y * CORES)])


def sort_slots(row, shard, half, live):
    index = jnp.arange(row.shape[0], dtype=I32)
    late = shard >= EARLY
    kind = jnp.where(index < live, late.astype(I32), 2)
    key = kind * row.shape[0] + index
    rank = jnp.sum(key[None, :] < key[:, None], axis=1)
    tile = jnp.where(late, shard - EARLY, shard) * 2 + half
    lists = jnp.stack([row, tile, index])
    spread = jnp.sum(jnp.where(rank[None, :] == index[:, None], lists[:, None, :], 0), axis=2)
    ends = jnp.stack([jnp.sum(kind == 0), live])
    return jnp.concatenate([spread, jnp.broadcast_to(ends[:, None], (2, row.shape[0]))])


def body(
    node_features, neighbour_count, tile_rows, tile_cols, tile_count, patterns, w_self, w_neigh, bias
):
    row_tiles = Y * CORES * SPAN // TILE
    mine = project(node_features, w_neigh)

    far = from_far_z(mine)
    line = jnp.concatenate([mine] + [from_step(mine, step, 0) for step in STEPS[1:]])
    across = [from_step(line, step, 1) for step in STEPS[1:]]
    zero_one, zero = load_patterns(patterns[0, 0], line)
    far_line = jnp.concatenate([far] + [from_step(far, step, 0) for step in STEPS[1:]]) + zero[0, 0]
    far_across = [from_step(far_line, step, 1) for step in STEPS[1:]]

    row_at, col_at = lax.axis_index("row"), lax.axis_index("col")
    z_at, x_at = row_at // X, row_at % X
    y_at, core_at = col_at // CORES, col_at % CORES
    cols = tile_cols[0, 0]
    source = cols // 2
    dz = (source // X - z_at) % Z
    dx = (source % X - x_at) % X
    x_place = jnp.where(dx == 3, 2, jnp.where(dx == 2, 3, dx))
    z_step = dz % 4
    z_place = jnp.where(z_step == 3, 2, jnp.where(z_step == 2, 3, z_step))
    first = jnp.where(z_place == 2, 7, jnp.where((z_place == 3) & (z_at % 2 == 1), 6, z_step))
    second = dz != first
    z_first = core_at == 1
    line_place, across_place = jnp.where(z_first, z_place, x_place), jnp.where(z_first, x_place, z_place)
    piece = jnp.where(across_place == 0, second.astype(I32), across_place + jnp.where(second, 4, 1))
    shard = piece * 4 + line_place
    rows = tile_rows[0, 0]
    span = rows // 2
    other = (span % CORES != core_at).astype(I32)
    row_index = other * (row_tiles // 2) + ((span // CORES - y_at) % Y) * 2 + rows % 2
    slots = sort_slots(row_index, shard, cols % 2, tile_count[0, 0])

    early = aggregate(slots, zero_one, [line, far_line, *across], row_tiles)
    keep, send = aggregate(slots, zero_one, far_across, row_tiles, early)

    own, *pays = add_pair(keep, from_core(send))
    pays = [from_y(pay, -j) for j, pay in enumerate(pays, 1)]
    self_rows = self_part(node_features, w_self, bias[None, :])
    return finish(own, self_rows, neighbour_count.reshape(SPAN // LANES, LANES), pays)


def solution(mesh):
    return jax.shard_map(
        body,
        mesh=mesh,
        in_specs=(
            P(("row", "col"), None),
            P(("row", "col")),
            P("row", "col", None),
            P("row", "col", None),
            P("row", "col"),
            P("row", "col", None, None, None),
            P(),
            P(),
            P(),
        ),
        out_specs=P(("row", "col"), None),
        check_vma=False,
    )
```

```python
import functools

import jax
import jax.numpy as jnp
from jax import lax
from jax.experimental import pallas as pl
from jax.experimental.pallas import tpu as pltpu
from jax.sharding import PartitionSpec as P

Z, X, Y, CORES = 8, 4, 4, 2
SPAN = 256
TILE = 128
H = 256
LANES = 128
WORDS = H // 2
SHARD = SPAN + 8
GROUP = 16
CHUNKS = 3
EARLY = 20
STEPS = (0, 1, -1, 2)
VMEM_LIMIT = 20 * 1024 * 1024
BF, F32, I32 = jnp.bfloat16, jnp.float32, jnp.int32


def encode(values, out_ref):
    size = jnp.maximum(jnp.max(jnp.abs(values), axis=1, keepdims=True), 2.0**-100)
    exponent = jnp.floor(jnp.log2(size) + 0.001)
    codes = jnp.floor(values * jnp.exp2(14.0 - exponent) + 0.5).astype(I32)
    out_ref[:SPAN, :] = (codes[:, :WORDS] << 16) | (codes[:, WORDS:] & 0xFFFF)
    along = jnp.transpose(jnp.broadcast_to(exponent, (SPAN, LANES))).astype(I32)
    out_ref[SPAN : SPAN + 8, :] = jnp.zeros((8, LANES), I32)
    for half in range(SPAN // LANES):
        out_ref[SPAN + half : SPAN + half + 1, :] = along[:1, half * LANES : (half + 1) * LANES]


def power_of_two(exponent):
    left = exponent + (120 - 14)
    result = jnp.full(exponent.shape, 2.0**-120, F32)
    for bit in range(7):
        result = jnp.where((left >> bit) & 1 == 1, result * 2.0 ** (1 << bit), result)
    return jnp.where((left >> 7) & 1 == 1, result * 2.0**64 * 2.0**64, result)


def two_codes(words):
    return (words >> 16).astype(F32), ((words << 16) >> 16).astype(F32)


def vmem(*arrays):
    return [pltpu.with_memory_space_constraint(array, pltpu.VMEM) for array in arrays]


IN_VMEM = pl.BlockSpec(memory_space=pltpu.VMEM)


def project_kernel(x_hbm, w_hbm, out_ref, x_ref, w_ref, sem):
    chunk = x_ref.shape[1] // CHUNKS
    copies = []
    for n in range(CHUNKS):
        at = pl.ds(n * chunk, chunk)
        copies.append(pltpu.make_async_copy(w_hbm.at[at], w_ref.at[at], sem.at[n]))
        copies.append(pltpu.make_async_copy(x_hbm.at[:, at], x_ref.at[:, at], sem.at[CHUNKS + n]))
    for copy in copies:
        copy.start()
    z = jnp.zeros((SPAN, H), F32)
    for n in range(CHUNKS):
        copies[2 * n].wait()
        copies[2 * n + 1].wait()
        at = slice(n * chunk, (n + 1) * chunk)
        w = w_ref[at]
        high = w.astype(BF)
        low = (w - high.astype(F32)).astype(BF)
        x = x_ref[:, at]
        z += jnp.dot(x, high, preferred_element_type=F32) + jnp.dot(x, low, preferred_element_type=F32)
    encode(z, out_ref)


def project(x, w):
    return pl.pallas_call(
        project_kernel,
        out_shape=pltpu.VMEM((SHARD, WORDS), I32),
        in_specs=[pl.BlockSpec(memory_space=pltpu.HBM)] * 2,
        out_specs=IN_VMEM,
        scratch_shapes=[
            pltpu.VMEM(x.shape, x.dtype),
            pltpu.VMEM(w.shape, w.dtype),
            pltpu.SemaphoreType.DMA((2 * CHUNKS,)),
        ],
        compiler_params=pltpu.CompilerParams(vmem_limit_bytes=VMEM_LIMIT),
        name="project",
    )(*[pltpu.with_memory_space_constraint(array, pltpu.HBM) for array in (x, w)])


def zero_kernel(after_ref, zero_ref):
    zero_ref[...] = after_ref[SPAN + 2 : SPAN + 3, :1]


def zero_after(blocks):
    return pl.pallas_call(
        zero_kernel,
        out_shape=pltpu.VMEM((1, 1), I32),
        in_specs=[IN_VMEM],
        out_specs=IN_VMEM,
        name="zero_after",
    )(*vmem(blocks))


def load_kernel(pat_hbm, after_ref, out_ref, landing, sem):
    chunk, depth = landing.shape[1], landing.shape[0]
    steps = pat_hbm.shape[0] // chunk

    def fetch(step):
        slot = step % depth
        return pltpu.make_async_copy(pat_hbm.at[pl.ds(step * chunk, chunk)], landing.at[slot], sem.at[slot])

    for step in range(depth):
        fetch(step).start()
    for step in range(steps):
        fetch(step).wait()
        out_ref[step * chunk : (step + 1) * chunk] = landing[step % depth].astype(BF)
        if step + depth < steps:
            fetch(step + depth).start()


def load_patterns(patterns, after):
    return pl.pallas_call(
        load_kernel,
        out_shape=pltpu.VMEM(patterns.shape, BF),
        in_specs=[pl.BlockSpec(memory_space=pltpu.HBM), IN_VMEM],
        out_specs=IN_VMEM,
        scratch_shapes=[pltpu.VMEM((8, 8, TILE, TILE), I32), pltpu.SemaphoreType.DMA((8,))],
        compiler_params=pltpu.CompilerParams(vmem_limit_bytes=VMEM_LIMIT),
        name="load_patterns",
    )(pltpu.with_memory_space_constraint(patterns, pltpu.HBM), *vmem(after))


def aggregate_kernel(late, counts, slots_ref, pat, *refs):
    pieces, refs = refs[: len(counts)], refs[len(counts) :]
    if late:
        first_ref, keep_ref, send_ref, parts, scales, acc = refs
    else:
        acc, parts, scales = refs
    start = slots_ref[3, 0] if late else 0
    stop = slots_ref[4, 0] if late else slots_ref[3, 0]
    groups = (stop - start + GROUP - 1) // GROUP

    acc[...] = first_ref[...] if late else jnp.zeros_like(acc)

    at = 0
    for piece, count in zip(pieces, counts):

        def decode(n, carry, piece=piece, at=at):
            base = pl.multiple_of(n * SHARD, 8)
            scale = power_of_two(piece[pl.ds(base + SPAN, 8), :])
            for half in range(2):
                words = piece[pl.ds(base + half * TILE, TILE), :]
                tile = (at + n) * 2 + half
                scales[tile] = jnp.broadcast_to(scale[half : half + 1], (8, LANES))
                for side, code in enumerate(two_codes(words)):
                    high = code.astype(BF)
                    low = (code - high.astype(F32)).astype(BF)
                    where = pl.ds(side * WORDS, WORDS)
                    parts[tile, :TILE, where] = high
                    parts[tile, TILE:, where] = low
            return carry

        lax.fori_loop(0, count, decode, 0)
        at += count

    def add_group(g, carry):
        for k in range(GROUP):
            n = start + g * GROUP + k
            at = jnp.minimum(n, pat.shape[0] - 1)
            row, col = slots_ref[0, at], jnp.where(n < stop, slots_ref[1, at], 0)
            p = pat[slots_ref[2, at]] * jnp.where(n < stop, scales[col], 0.0)[:1].astype(BF)
            acc[row] += jnp.dot(
                jnp.concatenate([p, p], axis=1), parts[col], preferred_element_type=F32
            )
        return carry

    lax.fori_loop(0, groups, add_group, 0)
    if late:
        keep_ref[...] = acc[: acc.shape[0] // 2]
        send_ref[...] = acc[acc.shape[0] // 2 :]


def aggregate(slots, pat, pieces, row_tiles, first=None):
    late = first is not None
    counts = tuple(piece.shape[0] // SHARD for piece in pieces)
    shards = sum(counts)
    sums = pltpu.VMEM((row_tiles, TILE, H), F32)
    half = pltpu.VMEM((row_tiles // 2, TILE, H), F32)
    operands = vmem(pat, *pieces, first) if late else vmem(pat, *pieces)
    return pl.pallas_call(
        functools.partial(aggregate_kernel, late, counts),
        out_shape=[half, half] if late else sums,
        in_specs=[pl.BlockSpec(memory_space=pltpu.SMEM)] + [IN_VMEM] * len(operands),
        out_specs=[IN_VMEM, IN_VMEM] if late else IN_VMEM,
        scratch_shapes=[
            pltpu.VMEM((shards * 2, 2 * TILE, H), BF),
            pltpu.VMEM((shards * 2, 8, LANES), F32),
        ]
        + [sums] * late,
        compiler_params=pltpu.CompilerParams(vmem_limit_bytes=VMEM_LIMIT),
        name="aggregate_late" if late else "aggregate_early",
    )(slots, *operands)


def pair_kernel(keep_ref, other_ref, own_ref, *pay_refs):
    tiles = SPAN // TILE
    for j in range(Y):
        at = pl.ds(j * tiles, tiles)
        both = (keep_ref[at] + other_ref[at]).reshape(SPAN, H)
        if j == 0:
            own_ref[...] = both
        else:
            encode(both, pay_refs[j - 1])


def add_pair(keep, other):
    return pl.pallas_call(
        pair_kernel,
        out_shape=[pltpu.VMEM((SPAN, H), F32)] + [pltpu.VMEM((SHARD, WORDS), I32)] * (Y - 1),
        in_specs=[IN_VMEM] * 2,
        out_specs=[IN_VMEM] * Y,
        compiler_params=pltpu.CompilerParams(vmem_limit_bytes=VMEM_LIMIT),
        name="add_pair",
    )(*vmem(keep, other))


def self_kernel(x_ref, w_ref, bias_ref, out_ref):
    w = w_ref[...]
    high = w.astype(BF)
    low = (w - high.astype(F32)).astype(BF)
    x = x_ref[...]
    z = jnp.dot(x, high, preferred_element_type=F32) + jnp.dot(x, low, preferred_element_type=F32)
    out_ref[...] = z + bias_ref[...]


def self_part(x, w, bias):
    return pl.pallas_call(
        self_kernel,
        out_shape=pltpu.VMEM((SPAN, H), F32),
        out_specs=IN_VMEM,
        compiler_params=pltpu.CompilerParams(vmem_limit_bytes=VMEM_LIMIT),
        name="self_part",
    )(x, w, bias)


def finish_kernel(own_ref, self_ref, count_ref, *refs):
    out_ref = refs[-1]
    for half in range(SPAN // TILE):
        at = pl.ds(half * TILE, TILE)
        left, right = own_ref[at, :WORDS], own_ref[at, WORDS:]
        for pay_ref in refs[:-1]:
            row = pay_ref[SPAN + half : SPAN + half + 1, :]
            scale = jnp.transpose(jnp.broadcast_to(power_of_two(row), (TILE, LANES)))
            a, b = two_codes(pay_ref[at, :])
            left, right = left + a * scale, right + b * scale
        d = jnp.transpose(jnp.broadcast_to(count_ref[half : half + 1].astype(F32), (TILE, LANES)))
        out_ref[at, :WORDS] = jnp.maximum(left / d + self_ref[at, :WORDS], 0.0)
        out_ref[at, WORDS:] = jnp.maximum(right / d + self_ref[at, WORDS:], 0.0)


def finish(own, self_rows, count, pays):
    return pl.pallas_call(
        finish_kernel,
        out_shape=jax.ShapeDtypeStruct((SPAN, H), F32),
        compiler_params=pltpu.CompilerParams(vmem_limit_bytes=VMEM_LIMIT),
        in_specs=[IN_VMEM] * (3 + len(pays)),
        name="finish",
    )(*vmem(own, self_rows), count, *vmem(*pays))


def from_far_z(x):
    return lax.ppermute(x, "row", [(((z + Z // 2) % Z) * X + k, z * X + k) for z in range(Z) for k in range(X)])


def from_step(x, step, x_core):
    pairs = []
    for z in range(Z):
        for k in range(X):
            for c in range(Y * CORES):
                if c % CORES == x_core:
                    source = z * X + (k + step) % X
                else:
                    source = ((z + (-step if step == 2 and z % 2 else step)) % Z) * X + k
                pairs.append((source * Y * CORES + c, (z * X + k) * Y * CORES + c))
    return lax.ppermute(x, ("row", "col"), pairs)


def from_y(x, d):
    return lax.ppermute(
        x, "col", [(((y + d) % Y) * CORES + k, y * CORES + k) for y in range(Y) for k in range(CORES)]
    )


def from_core(x):
    return lax.ppermute(x, "col", [(c ^ 1, c) for c in range(Y * CORES)])


def sort_slots(row, shard, half, live):
    index = jnp.arange(row.shape[0], dtype=I32)
    late = shard >= EARLY
    kind = jnp.where(index < live, late.astype(I32), 2)
    key = kind * row.shape[0] + index
    rank = jnp.sum(key[None, :] < key[:, None], axis=1)
    tile = jnp.where(late, shard - EARLY, shard) * 2 + half
    lists = jnp.stack([row, tile, index])
    spread = jnp.sum(jnp.where(rank[None, :] == index[:, None], lists[:, None, :], 0), axis=2)
    ends = jnp.stack([jnp.sum(kind == 0), live])
    return jnp.concatenate([spread, jnp.broadcast_to(ends[:, None], (2, row.shape[0]))])


def body(
    node_features, neighbour_count, tile_rows, tile_cols, tile_count, patterns, w_self, w_neigh, bias
):
    row_tiles = Y * CORES * SPAN // TILE
    mine = project(node_features, w_neigh)

    line = jnp.concatenate([mine] + [from_step(mine, step, 0) for step in STEPS[1:]])
    far = from_far_z(mine)
    across = [from_step(line, step, 1) for step in STEPS[1:]]
    zero = zero_after(line)
    far_line = jnp.concatenate([far] + [from_step(far, step, 0) for step in STEPS[1:]]) + zero[0, 0]
    far_across = [from_step(far_line, step, 1) for step in STEPS[1:]]
    zero_one = load_patterns(patterns[0, 0], far_line)

    row_at, col_at = lax.axis_index("row"), lax.axis_index("col")
    z_at, x_at = row_at // X, row_at % X
    y_at, core_at = col_at // CORES, col_at % CORES
    cols = tile_cols[0, 0] + far_line[-1, -1]
    source = cols // 2
    dz = (source // X - z_at) % Z
    dx = (source % X - x_at) % X
    x_place = jnp.where(dx == 3, 2, jnp.where(dx == 2, 3, dx))
    z_step = dz % 4
    z_place = jnp.where(z_step == 3, 2, jnp.where(z_step == 2, 3, z_step))
    first = jnp.where(z_place == 2, 7, jnp.where((z_place == 3) & (z_at % 2 == 1), 6, z_step))
    second = dz != first
    z_first = core_at == 1
    line_place, across_place = jnp.where(z_first, z_place, x_place), jnp.where(z_first, x_place, z_place)
    piece = jnp.where(across_place == 0, second.astype(I32), across_place + jnp.where(second, 4, 1))
    shard = piece * 4 + line_place
    rows = tile_rows[0, 0]
    span = rows // 2
    other = (span % CORES != core_at).astype(I32)
    row_index = other * (row_tiles // 2) + ((span // CORES - y_at) % Y) * 2 + rows % 2
    slots = sort_slots(row_index, shard, cols % 2, tile_count[0, 0])

    early = aggregate(slots, zero_one, [line, far_line, *across], row_tiles)
    keep, send = aggregate(slots, zero_one, far_across, row_tiles, early)

    own, *pays = add_pair(keep, from_core(send))
    pays = [from_y(pays[j - 1], -j) for j in (2, 1, 3)]
    self_rows = self_part(node_features, w_self, bias[None, :])
    return finish(own, self_rows, neighbour_count.reshape(SPAN // LANES, LANES), pays)


def solution(mesh):
    return jax.shard_map(
        body,
        mesh=mesh,
        in_specs=(
            P(("row", "col"), None),
            P(("row", "col")),
            P("row", "col", None),
            P("row", "col", None),
            P("row", "col"),
            P("row", "col", None, None, None),
            P(),
            P(),
            P(),
        ),
        out_specs=P(("row", "col"), None),
        check_vma=False,
    )
```

```python
import functools

import jax
import jax.numpy as jnp
from jax import lax
from jax.experimental import pallas as pl
from jax.experimental.pallas import tpu as pltpu
from jax.sharding import PartitionSpec as P

Z, X, Y, CORES = 8, 4, 4, 2
SPAN = 256
TILE = 128
H = 256
LANES = 128
WORDS = H // 2
SHARD = SPAN + 8
GROUP = 16
CHUNKS = 3
EARLY = 20
STEPS = (0, 1, -1, 2)
VMEM_LIMIT = 20 * 1024 * 1024
BF, F32, I32 = jnp.bfloat16, jnp.float32, jnp.int32


def encode(values, out_ref):
    size = jnp.maximum(jnp.max(jnp.abs(values), axis=1, keepdims=True), 2.0**-100)
    exponent = jnp.floor(jnp.log2(size) + 0.001)
    codes = jnp.floor(values * jnp.exp2(14.0 - exponent) + 0.5).astype(I32)
    out_ref[:SPAN, :] = (codes[:, :WORDS] << 16) | (codes[:, WORDS:] & 0xFFFF)
    along = jnp.transpose(jnp.broadcast_to(exponent, (SPAN, LANES))).astype(I32)
    out_ref[SPAN : SPAN + 8, :] = jnp.zeros((8, LANES), I32)
    for half in range(SPAN // LANES):
        out_ref[SPAN + half : SPAN + half + 1, :] = along[:1, half * LANES : (half + 1) * LANES]


def power_of_two(exponent):
    left = exponent + (120 - 14)
    result = jnp.full(exponent.shape, 2.0**-120, F32)
    for bit in range(7):
        result = jnp.where((left >> bit) & 1 == 1, result * 2.0 ** (1 << bit), result)
    return jnp.where((left >> 7) & 1 == 1, result * 2.0**64 * 2.0**64, result)


def two_codes(words):
    return (words >> 16).astype(F32), ((words << 16) >> 16).astype(F32)


def vmem(*arrays):
    return [pltpu.with_memory_space_constraint(array, pltpu.VMEM) for array in arrays]


IN_VMEM = pl.BlockSpec(memory_space=pltpu.VMEM)


def project_kernel(x_hbm, w_hbm, out_ref, x_ref, w_ref, sem):
    chunk = x_ref.shape[1] // CHUNKS
    copies = []
    for n in range(CHUNKS):
        at = pl.ds(n * chunk, chunk)
        copies.append(pltpu.make_async_copy(w_hbm.at[at], w_ref.at[at], sem.at[n]))
        copies.append(pltpu.make_async_copy(x_hbm.at[:, at], x_ref.at[:, at], sem.at[CHUNKS + n]))
    for copy in copies:
        copy.start()
    z = jnp.zeros((SPAN, H), F32)
    for n in range(CHUNKS):
        copies[2 * n].wait()
        copies[2 * n + 1].wait()
        at = slice(n * chunk, (n + 1) * chunk)
        w = w_ref[at]
        high = w.astype(BF)
        low = (w - high.astype(F32)).astype(BF)
        x = x_ref[:, at]
        z += jnp.dot(x, high, preferred_element_type=F32) + jnp.dot(x, low, preferred_element_type=F32)
    encode(z, out_ref)


def project(x, w):
    return pl.pallas_call(
        project_kernel,
        out_shape=pltpu.VMEM((SHARD, WORDS), I32),
        in_specs=[pl.BlockSpec(memory_space=pltpu.HBM)] * 2,
        out_specs=IN_VMEM,
        scratch_shapes=[
            pltpu.VMEM(x.shape, x.dtype),
            pltpu.VMEM(w.shape, w.dtype),
            pltpu.SemaphoreType.DMA((2 * CHUNKS,)),
        ],
        compiler_params=pltpu.CompilerParams(vmem_limit_bytes=VMEM_LIMIT),
        name="project",
    )(*[pltpu.with_memory_space_constraint(array, pltpu.HBM) for array in (x, w)])


def zero_kernel(after_ref, zero_ref):
    zero_ref[...] = after_ref[SPAN + 2 : SPAN + 3, :1]


def zero_after(blocks):
    return pl.pallas_call(
        zero_kernel,
        out_shape=pltpu.VMEM((1, 1), I32),
        in_specs=[IN_VMEM],
        out_specs=IN_VMEM,
        name="zero_after",
    )(*vmem(blocks))


def load_kernel(pat_hbm, after_ref, out_ref, zero_ref, landing, sem):
    zero_ref[...] = after_ref[SPAN + 2 : SPAN + 3, :1]
    chunk, depth = landing.shape[1], landing.shape[0]
    steps = pat_hbm.shape[0] // chunk

    def fetch(step):
        slot = step % depth
        return pltpu.make_async_copy(pat_hbm.at[pl.ds(step * chunk, chunk)], landing.at[slot], sem.at[slot])

    for step in range(depth):
        fetch(step).start()
    for step in range(steps):
        fetch(step).wait()
        out_ref[step * chunk : (step + 1) * chunk] = landing[step % depth].astype(BF)
        if step + depth < steps:
            fetch(step + depth).start()


def load_patterns(patterns, after):
    return pl.pallas_call(
        load_kernel,
        out_shape=[pltpu.VMEM(patterns.shape, BF), pltpu.VMEM((1, 1), I32)],
        in_specs=[pl.BlockSpec(memory_space=pltpu.HBM), IN_VMEM],
        out_specs=[IN_VMEM, IN_VMEM],
        scratch_shapes=[pltpu.VMEM((8, 8, TILE, TILE), I32), pltpu.SemaphoreType.DMA((8,))],
        compiler_params=pltpu.CompilerParams(vmem_limit_bytes=VMEM_LIMIT),
        name="load_patterns",
    )(pltpu.with_memory_space_constraint(patterns, pltpu.HBM), *vmem(after))


def aggregate_kernel(late, counts, slots_ref, pat, *refs):
    pieces, refs = refs[: len(counts)], refs[len(counts) :]
    if late:
        first_ref, keep_ref, send_ref, parts, scales, acc = refs
    else:
        acc, parts, scales = refs
    start = slots_ref[3, 0] if late else 0
    stop = slots_ref[4, 0] if late else slots_ref[3, 0]
    groups = (stop - start + GROUP - 1) // GROUP

    acc[...] = first_ref[...] if late else jnp.zeros_like(acc)

    at = 0
    for piece, count in zip(pieces, counts):

        def decode(n, carry, piece=piece, at=at):
            base = pl.multiple_of(n * SHARD, 8)
            scale = power_of_two(piece[pl.ds(base + SPAN, 8), :])
            for half in range(2):
                words = piece[pl.ds(base + half * TILE, TILE), :]
                tile = (at + n) * 2 + half
                scales[tile] = jnp.broadcast_to(scale[half : half + 1], (8, LANES))
                for side, code in enumerate(two_codes(words)):
                    high = code.astype(BF)
                    low = (code - high.astype(F32)).astype(BF)
                    where = pl.ds(side * WORDS, WORDS)
                    parts[tile, :TILE, where] = high
                    parts[tile, TILE:, where] = low
            return carry

        lax.fori_loop(0, count, decode, 0)
        at += count

    def add_group(g, carry):
        for k in range(GROUP):
            n = start + g * GROUP + k
            at = jnp.minimum(n, pat.shape[0] - 1)
            row, col = slots_ref[0, at], jnp.where(n < stop, slots_ref[1, at], 0)
            p = pat[slots_ref[2, at]] * jnp.where(n < stop, scales[col], 0.0)[:1].astype(BF)
            acc[row] += jnp.dot(
                jnp.concatenate([p, p], axis=1), parts[col], preferred_element_type=F32
            )
        return carry

    lax.fori_loop(0, groups, add_group, 0)
    if late:
        keep_ref[...] = acc[: acc.shape[0] // 2]
        send_ref[...] = acc[acc.shape[0] // 2 :]


def aggregate(slots, pat, pieces, row_tiles, first=None):
    late = first is not None
    counts = tuple(piece.shape[0] // SHARD for piece in pieces)
    shards = sum(counts)
    sums = pltpu.VMEM((row_tiles, TILE, H), F32)
    half = pltpu.VMEM((row_tiles // 2, TILE, H), F32)
    operands = vmem(pat, *pieces, first) if late else vmem(pat, *pieces)
    return pl.pallas_call(
        functools.partial(aggregate_kernel, late, counts),
        out_shape=[half, half] if late else sums,
        in_specs=[pl.BlockSpec(memory_space=pltpu.SMEM)] + [IN_VMEM] * len(operands),
        out_specs=[IN_VMEM, IN_VMEM] if late else IN_VMEM,
        scratch_shapes=[
            pltpu.VMEM((shards * 2, 2 * TILE, H), BF),
            pltpu.VMEM((shards * 2, 8, LANES), F32),
        ]
        + [sums] * late,
        compiler_params=pltpu.CompilerParams(vmem_limit_bytes=VMEM_LIMIT),
        name="aggregate_late" if late else "aggregate_early",
    )(slots, *operands)


def pair_kernel(keep_ref, other_ref, own_ref, *pay_refs):
    tiles = SPAN // TILE
    for j in range(Y):
        at = pl.ds(j * tiles, tiles)
        both = (keep_ref[at] + other_ref[at]).reshape(SPAN, H)
        if j == 0:
            own_ref[...] = both
        else:
            encode(both, pay_refs[j - 1])


def add_pair(keep, other):
    return pl.pallas_call(
        pair_kernel,
        out_shape=[pltpu.VMEM((SPAN, H), F32)] + [pltpu.VMEM((SHARD, WORDS), I32)] * (Y - 1),
        in_specs=[IN_VMEM] * 2,
        out_specs=[IN_VMEM] * Y,
        compiler_params=pltpu.CompilerParams(vmem_limit_bytes=VMEM_LIMIT),
        name="add_pair",
    )(*vmem(keep, other))


def self_kernel(x_ref, w_ref, bias_ref, out_ref):
    w = w_ref[...]
    high = w.astype(BF)
    low = (w - high.astype(F32)).astype(BF)
    x = x_ref[...]
    z = jnp.dot(x, high, preferred_element_type=F32) + jnp.dot(x, low, preferred_element_type=F32)
    out_ref[...] = z + bias_ref[...]


def self_part(x, w, bias):
    return pl.pallas_call(
        self_kernel,
        out_shape=pltpu.VMEM((SPAN, H), F32),
        out_specs=IN_VMEM,
        compiler_params=pltpu.CompilerParams(vmem_limit_bytes=VMEM_LIMIT),
        name="self_part",
    )(x, w, bias)


def finish_kernel(own_ref, self_ref, count_ref, *refs):
    out_ref = refs[-1]
    for half in range(SPAN // TILE):
        at = pl.ds(half * TILE, TILE)
        left, right = own_ref[at, :WORDS], own_ref[at, WORDS:]
        for pay_ref in refs[:-1]:
            row = pay_ref[SPAN + half : SPAN + half + 1, :]
            scale = jnp.transpose(jnp.broadcast_to(power_of_two(row), (TILE, LANES)))
            a, b = two_codes(pay_ref[at, :])
            left, right = left + a * scale, right + b * scale
        d = jnp.transpose(jnp.broadcast_to(count_ref[half : half + 1].astype(F32), (TILE, LANES)))
        out_ref[at, :WORDS] = jnp.maximum(left / d + self_ref[at, :WORDS], 0.0)
        out_ref[at, WORDS:] = jnp.maximum(right / d + self_ref[at, WORDS:], 0.0)


def finish(own, self_rows, count, pays):
    return pl.pallas_call(
        finish_kernel,
        out_shape=jax.ShapeDtypeStruct((SPAN, H), F32),
        compiler_params=pltpu.CompilerParams(vmem_limit_bytes=VMEM_LIMIT),
        in_specs=[IN_VMEM] * (3 + len(pays)),
        name="finish",
    )(*vmem(own, self_rows), count, *vmem(*pays))


def from_far_z(x):
    return lax.ppermute(x, "row", [(((z + Z // 2) % Z) * X + k, z * X + k) for z in range(Z) for k in range(X)])


def from_step(x, step, x_core):
    pairs = []
    for z in range(Z):
        for k in range(X):
            for c in range(Y * CORES):
                if c % CORES == x_core:
                    source = z * X + (k + step) % X
                else:
                    source = ((z + (-step if step == 2 and z % 2 else step)) % Z) * X + k
                pairs.append((source * Y * CORES + c, (z * X + k) * Y * CORES + c))
    return lax.ppermute(x, ("row", "col"), pairs)


def from_y(x, d):
    return lax.ppermute(
        x, "col", [(((y + d) % Y) * CORES + k, y * CORES + k) for y in range(Y) for k in range(CORES)]
    )


def from_core(x):
    return lax.ppermute(x, "col", [(c ^ 1, c) for c in range(Y * CORES)])


def sort_slots(row, shard, half, live):
    index = jnp.arange(row.shape[0], dtype=I32)
    late = shard >= EARLY
    kind = jnp.where(index < live, late.astype(I32), 2)
    key = kind * row.shape[0] + index
    rank = jnp.sum(key[None, :] < key[:, None], axis=1)
    tile = jnp.where(late, shard - EARLY, shard) * 2 + half
    lists = jnp.stack([row, tile, index])
    spread = jnp.sum(jnp.where(rank[None, :] == index[:, None], lists[:, None, :], 0), axis=2)
    ends = jnp.stack([jnp.sum(kind == 0), live])
    return jnp.concatenate([spread, jnp.broadcast_to(ends[:, None], (2, row.shape[0]))])


def body(
    node_features, neighbour_count, tile_rows, tile_cols, tile_count, patterns, w_self, w_neigh, bias
):
    row_tiles = Y * CORES * SPAN // TILE
    mine = project(node_features, w_neigh)

    line = jnp.concatenate([mine] + [from_step(mine, step, 0) for step in STEPS[1:]])
    far = from_far_z(mine)
    across = [from_step(line, step, 1) for step in STEPS[1:]]
    zero = zero_after(line)
    far_line = jnp.concatenate([far] + [from_step(far, step, 0) for step in STEPS[1:]]) + zero[0, 0]
    far_across = [from_step(far_line, step, 1) for step in STEPS[1:]]
    zero_one, late_zero = load_patterns(patterns[0, 0], far_line)

    row_at, col_at = lax.axis_index("row"), lax.axis_index("col")
    z_at, x_at = row_at // X, row_at % X
    y_at, core_at = col_at // CORES, col_at % CORES
    cols = tile_cols[0, 0] + late_zero[0, 0]
    source = cols // 2
    dz = (source // X - z_at) % Z
    dx = (source % X - x_at) % X
    x_place = jnp.where(dx == 3, 2, jnp.where(dx == 2, 3, dx))
    z_step = dz % 4
    z_place = jnp.where(z_step == 3, 2, jnp.where(z_step == 2, 3, z_step))
    first = jnp.where(z_place == 2, 7, jnp.where((z_place == 3) & (z_at % 2 == 1), 6, z_step))
    second = dz != first
    z_first = core_at == 1
    line_place, across_place = jnp.where(z_first, z_place, x_place), jnp.where(z_first, x_place, z_place)
    piece = jnp.where(across_place == 0, second.astype(I32), across_place + jnp.where(second, 4, 1))
    shard = piece * 4 + line_place
    rows = tile_rows[0, 0]
    span = rows // 2
    other = (span % CORES != core_at).astype(I32)
    row_index = other * (row_tiles // 2) + ((span // CORES - y_at) % Y) * 2 + rows % 2
    slots = sort_slots(row_index, shard, cols % 2, tile_count[0, 0])

    early = aggregate(slots, zero_one, [line, far_line, *across], row_tiles)
    keep, send = aggregate(slots, zero_one, far_across, row_tiles, early)

    own, *pays = add_pair(keep, from_core(send))
    pays = [from_y(pays[j - 1], -j) for j in (2, 1, 3)]
    self_rows = self_part(node_features, w_self, bias[None, :])
    return finish(own, self_rows, neighbour_count.reshape(SPAN // LANES, LANES), pays)


def solution(mesh):
    return jax.shard_map(
        body,
        mesh=mesh,
        in_specs=(
            P(("row", "col"), None),
            P(("row", "col")),
            P("row", "col", None),
            P("row", "col", None),
            P("row", "col"),
            P("row", "col", None, None, None),
            P(),
            P(),
            P(),
        ),
        out_specs=P(("row", "col"), None),
        check_vma=False,
    )
```

```python
import functools

import jax
import jax.numpy as jnp
from jax import lax
from jax.experimental import pallas as pl
from jax.experimental.pallas import tpu as pltpu
from jax.sharding import PartitionSpec as P

Z, X, Y, CORES = 8, 4, 4, 2
SPAN = 256
TILE = 128
H = 256
LANES = 128
WORDS = H // 2
SHARD = SPAN + 8
GROUP = 16
CHUNKS = 3
EARLY = 20
STEPS = (0, 1, -1, 2)
VMEM_LIMIT = 20 * 1024 * 1024
BF, F32, I32 = jnp.bfloat16, jnp.float32, jnp.int32


def encode(values, out_ref):
    size = jnp.maximum(jnp.max(jnp.abs(values), axis=1, keepdims=True), 2.0**-100)
    exponent = jnp.floor(jnp.log2(size) + 0.001)
    codes = jnp.floor(values * jnp.exp2(14.0 - exponent) + 0.5).astype(I32)
    out_ref[:SPAN, :] = (codes[:, :WORDS] << 16) | (codes[:, WORDS:] & 0xFFFF)
    along = jnp.transpose(jnp.broadcast_to(exponent, (SPAN, LANES))).astype(I32)
    out_ref[SPAN : SPAN + 8, :] = jnp.zeros((8, LANES), I32)
    for half in range(SPAN // LANES):
        out_ref[SPAN + half : SPAN + half + 1, :] = along[:1, half * LANES : (half + 1) * LANES]


def power_of_two(exponent):
    left = exponent + (120 - 14)
    result = jnp.full(exponent.shape, 2.0**-120, F32)
    for bit in range(7):
        result = jnp.where((left >> bit) & 1 == 1, result * 2.0 ** (1 << bit), result)
    return jnp.where((left >> 7) & 1 == 1, result * 2.0**64 * 2.0**64, result)


def two_codes(words):
    return (words >> 16).astype(F32), ((words << 16) >> 16).astype(F32)


def vmem(*arrays):
    return [pltpu.with_memory_space_constraint(array, pltpu.VMEM) for array in arrays]


IN_VMEM = pl.BlockSpec(memory_space=pltpu.VMEM)


def project_kernel(x_hbm, w_hbm, out_ref, x_ref, w_ref, sem):
    chunk = x_ref.shape[1] // CHUNKS
    copies = []
    for n in range(CHUNKS):
        at = pl.ds(n * chunk, chunk)
        copies.append(pltpu.make_async_copy(w_hbm.at[at], w_ref.at[at], sem.at[n]))
        copies.append(pltpu.make_async_copy(x_hbm.at[:, at], x_ref.at[:, at], sem.at[CHUNKS + n]))
    for copy in copies:
        copy.start()
    z = jnp.zeros((SPAN, H), F32)
    for n in range(CHUNKS):
        copies[2 * n].wait()
        copies[2 * n + 1].wait()
        at = slice(n * chunk, (n + 1) * chunk)
        w = w_ref[at]
        high = w.astype(BF)
        low = (w - high.astype(F32)).astype(BF)
        x = x_ref[:, at]
        z += jnp.dot(x, high, preferred_element_type=F32) + jnp.dot(x, low, preferred_element_type=F32)
    encode(z, out_ref)


def project(x, w):
    return pl.pallas_call(
        project_kernel,
        out_shape=pltpu.VMEM((SHARD, WORDS), I32),
        in_specs=[pl.BlockSpec(memory_space=pltpu.HBM)] * 2,
        out_specs=IN_VMEM,
        scratch_shapes=[
            pltpu.VMEM(x.shape, x.dtype),
            pltpu.VMEM(w.shape, w.dtype),
            pltpu.SemaphoreType.DMA((2 * CHUNKS,)),
        ],
        compiler_params=pltpu.CompilerParams(vmem_limit_bytes=VMEM_LIMIT),
        name="project",
    )(*[pltpu.with_memory_space_constraint(array, pltpu.HBM) for array in (x, w)])


def zero_kernel(after_ref, zero_ref):
    zero_ref[...] = after_ref[SPAN + 2 : SPAN + 3, :1]


def zero_after(blocks):
    return pl.pallas_call(
        zero_kernel,
        out_shape=pltpu.VMEM((1, 1), I32),
        in_specs=[IN_VMEM],
        out_specs=IN_VMEM,
        name="zero_after",
    )(*vmem(blocks))


def load_kernel(pat_hbm, after_ref, out_ref, zero_ref, landing, sem):
    zero_ref[...] = after_ref[SPAN + 2 : SPAN + 3, :1]
    chunk, depth = landing.shape[1], landing.shape[0]
    steps = pat_hbm.shape[0] // chunk

    def fetch(step):
        slot = step % depth
        return pltpu.make_async_copy(pat_hbm.at[pl.ds(step * chunk, chunk)], landing.at[slot], sem.at[slot])

    for step in range(depth):
        fetch(step).start()
    for step in range(steps):
        fetch(step).wait()
        out_ref[step * chunk : (step + 1) * chunk] = landing[step % depth].astype(BF)
        if step + depth < steps:
            fetch(step + depth).start()


def load_patterns(patterns, after):
    return pl.pallas_call(
        load_kernel,
        out_shape=[pltpu.VMEM(patterns.shape, BF), pltpu.VMEM((1, 1), I32)],
        in_specs=[pl.BlockSpec(memory_space=pltpu.HBM), IN_VMEM],
        out_specs=[IN_VMEM, IN_VMEM],
        scratch_shapes=[pltpu.VMEM((8, 8, TILE, TILE), I32), pltpu.SemaphoreType.DMA((8,))],
        compiler_params=pltpu.CompilerParams(vmem_limit_bytes=VMEM_LIMIT),
        name="load_patterns",
    )(pltpu.with_memory_space_constraint(patterns, pltpu.HBM), *vmem(after))


def aggregate_kernel(late, counts, slots_ref, pat, *refs):
    pieces, refs = refs[: len(counts)], refs[len(counts) :]
    if late:
        first_ref, keep_ref, send_ref, parts, scales, acc = refs
    else:
        acc, parts, scales = refs
    start = slots_ref[3, 0] if late else 0
    stop = slots_ref[4, 0] if late else slots_ref[3, 0]
    groups = (stop - start + GROUP - 1) // GROUP

    acc[...] = first_ref[...] if late else jnp.zeros_like(acc)

    at = 0
    for piece, count in zip(pieces, counts):

        def decode(n, carry, piece=piece, at=at):
            base = pl.multiple_of(n * SHARD, 8)
            scale = power_of_two(piece[pl.ds(base + SPAN, 8), :])
            for half in range(2):
                words = piece[pl.ds(base + half * TILE, TILE), :]
                tile = (at + n) * 2 + half
                scales[tile] = jnp.broadcast_to(scale[half : half + 1], (8, LANES))
                for side, code in enumerate(two_codes(words)):
                    high = code.astype(BF)
                    low = (code - high.astype(F32)).astype(BF)
                    where = pl.ds(side * WORDS, WORDS)
                    parts[tile, :TILE, where] = high
                    parts[tile, TILE:, where] = low
            return carry

        lax.fori_loop(0, count, decode, 0, unroll=True)
        at += count

    def add_group(g, carry):
        for k in range(GROUP):
            n = start + g * GROUP + k
            at = jnp.minimum(n, pat.shape[0] - 1)
            row, col = slots_ref[0, at], jnp.where(n < stop, slots_ref[1, at], 0)
            p = pat[slots_ref[2, at]] * jnp.where(n < stop, scales[col], 0.0)[:1].astype(BF)
            acc[row] += jnp.dot(
                jnp.concatenate([p, p], axis=1), parts[col], preferred_element_type=F32
            )
        return carry

    lax.fori_loop(0, groups, add_group, 0)
    if late:
        keep_ref[...] = acc[: acc.shape[0] // 2]
        send_ref[...] = acc[acc.shape[0] // 2 :]


def aggregate(slots, pat, pieces, row_tiles, first=None):
    late = first is not None
    counts = tuple(piece.shape[0] // SHARD for piece in pieces)
    shards = sum(counts)
    sums = pltpu.VMEM((row_tiles, TILE, H), F32)
    half = pltpu.VMEM((row_tiles // 2, TILE, H), F32)
    operands = vmem(pat, *pieces, first) if late else vmem(pat, *pieces)
    return pl.pallas_call(
        functools.partial(aggregate_kernel, late, counts),
        out_shape=[half, half] if late else sums,
        in_specs=[pl.BlockSpec(memory_space=pltpu.SMEM)] + [IN_VMEM] * len(operands),
        out_specs=[IN_VMEM, IN_VMEM] if late else IN_VMEM,
        scratch_shapes=[
            pltpu.VMEM((shards * 2, 2 * TILE, H), BF),
            pltpu.VMEM((shards * 2, 8, LANES), F32),
        ]
        + [sums] * late,
        compiler_params=pltpu.CompilerParams(vmem_limit_bytes=VMEM_LIMIT),
        name="aggregate_late" if late else "aggregate_early",
    )(slots, *operands)


def pair_kernel(keep_ref, other_ref, own_ref, *pay_refs):
    tiles = SPAN // TILE
    for j in range(Y):
        at = pl.ds(j * tiles, tiles)
        both = (keep_ref[at] + other_ref[at]).reshape(SPAN, H)
        if j == 0:
            own_ref[...] = both
        else:
            encode(both, pay_refs[j - 1])


def add_pair(keep, other):
    return pl.pallas_call(
        pair_kernel,
        out_shape=[pltpu.VMEM((SPAN, H), F32)] + [pltpu.VMEM((SHARD, WORDS), I32)] * (Y - 1),
        in_specs=[IN_VMEM] * 2,
        out_specs=[IN_VMEM] * Y,
        compiler_params=pltpu.CompilerParams(vmem_limit_bytes=VMEM_LIMIT),
        name="add_pair",
    )(*vmem(keep, other))


def self_kernel(x_ref, w_ref, bias_ref, out_ref):
    w = w_ref[...]
    high = w.astype(BF)
    low = (w - high.astype(F32)).astype(BF)
    x = x_ref[...]
    z = jnp.dot(x, high, preferred_element_type=F32) + jnp.dot(x, low, preferred_element_type=F32)
    out_ref[...] = z + bias_ref[...]


def self_part(x, w, bias):
    return pl.pallas_call(
        self_kernel,
        out_shape=pltpu.VMEM((SPAN, H), F32),
        out_specs=IN_VMEM,
        compiler_params=pltpu.CompilerParams(vmem_limit_bytes=VMEM_LIMIT),
        name="self_part",
    )(x, w, bias)


def finish_kernel(own_ref, self_ref, count_ref, *refs):
    out_ref = refs[-1]
    for half in range(SPAN // TILE):
        at = pl.ds(half * TILE, TILE)
        left, right = own_ref[at, :WORDS], own_ref[at, WORDS:]
        for pay_ref in refs[:-1]:
            row = pay_ref[SPAN + half : SPAN + half + 1, :]
            scale = jnp.transpose(jnp.broadcast_to(power_of_two(row), (TILE, LANES)))
            a, b = two_codes(pay_ref[at, :])
            left, right = left + a * scale, right + b * scale
        d = jnp.transpose(jnp.broadcast_to(count_ref[half : half + 1].astype(F32), (TILE, LANES)))
        out_ref[at, :WORDS] = jnp.maximum(left / d + self_ref[at, :WORDS], 0.0)
        out_ref[at, WORDS:] = jnp.maximum(right / d + self_ref[at, WORDS:], 0.0)


def finish(own, self_rows, count, pays):
    return pl.pallas_call(
        finish_kernel,
        out_shape=jax.ShapeDtypeStruct((SPAN, H), F32),
        compiler_params=pltpu.CompilerParams(vmem_limit_bytes=VMEM_LIMIT),
        in_specs=[IN_VMEM] * (3 + len(pays)),
        name="finish",
    )(*vmem(own, self_rows), count, *vmem(*pays))


def from_far_z(x):
    return lax.ppermute(x, "row", [(((z + Z // 2) % Z) * X + k, z * X + k) for z in range(Z) for k in range(X)])


def from_step(x, step, x_core):
    pairs = []
    for z in range(Z):
        for k in range(X):
            for c in range(Y * CORES):
                if c % CORES == x_core:
                    source = z * X + (k + step) % X
                else:
                    source = ((z + (-step if step == 2 and z % 2 else step)) % Z) * X + k
                pairs.append((source * Y * CORES + c, (z * X + k) * Y * CORES + c))
    return lax.ppermute(x, ("row", "col"), pairs)


def from_y(x, d):
    return lax.ppermute(
        x, "col", [(((y + d) % Y) * CORES + k, y * CORES + k) for y in range(Y) for k in range(CORES)]
    )


def from_core(x):
    return lax.ppermute(x, "col", [(c ^ 1, c) for c in range(Y * CORES)])


def sort_slots(row, shard, half, live):
    index = jnp.arange(row.shape[0], dtype=I32)
    late = shard >= EARLY
    kind = jnp.where(index < live, late.astype(I32), 2)
    key = kind * row.shape[0] + index
    rank = jnp.sum(key[None, :] < key[:, None], axis=1)
    tile = jnp.where(late, shard - EARLY, shard) * 2 + half
    lists = jnp.stack([row, tile, index])
    spread = jnp.sum(jnp.where(rank[None, :] == index[:, None], lists[:, None, :], 0), axis=2)
    ends = jnp.stack([jnp.sum(kind == 0), live])
    return jnp.concatenate([spread, jnp.broadcast_to(ends[:, None], (2, row.shape[0]))])


def body(
    node_features, neighbour_count, tile_rows, tile_cols, tile_count, patterns, w_self, w_neigh, bias
):
    row_tiles = Y * CORES * SPAN // TILE
    mine = project(node_features, w_neigh)

    line = jnp.concatenate([mine] + [from_step(mine, step, 0) for step in STEPS[1:]])
    far = from_far_z(mine)
    across = [from_step(line, step, 1) for step in STEPS[1:]]
    zero = zero_after(line)
    far_line = jnp.concatenate([far] + [from_step(far, step, 0) for step in STEPS[1:]]) + zero[0, 0]
    far_across = [from_step(far_line, step, 1) for step in STEPS[1:]]
    zero_one, late_zero = load_patterns(patterns[0, 0], far_line)

    row_at, col_at = lax.axis_index("row"), lax.axis_index("col")
    z_at, x_at = row_at // X, row_at % X
    y_at, core_at = col_at // CORES, col_at % CORES
    cols = tile_cols[0, 0] + late_zero[0, 0]
    source = cols // 2
    dz = (source // X - z_at) % Z
    dx = (source % X - x_at) % X
    x_place = jnp.where(dx == 3, 2, jnp.where(dx == 2, 3, dx))
    z_step = dz % 4
    z_place = jnp.where(z_step == 3, 2, jnp.where(z_step == 2, 3, z_step))
    first = jnp.where(z_place == 2, 7, jnp.where((z_place == 3) & (z_at % 2 == 1), 6, z_step))
    second = dz != first
    z_first = core_at == 1
    line_place, across_place = jnp.where(z_first, z_place, x_place), jnp.where(z_first, x_place, z_place)
    piece = jnp.where(across_place == 0, second.astype(I32), across_place + jnp.where(second, 4, 1))
    shard = piece * 4 + line_place
    rows = tile_rows[0, 0]
    span = rows // 2
    other = (span % CORES != core_at).astype(I32)
    row_index = other * (row_tiles // 2) + ((span // CORES - y_at) % Y) * 2 + rows % 2
    slots = sort_slots(row_index, shard, cols % 2, tile_count[0, 0])

    early = aggregate(slots, zero_one, [line, far_line, *across], row_tiles)
    keep, send = aggregate(slots, zero_one, far_across, row_tiles, early)

    own, *pays = add_pair(keep, from_core(send))
    pays = [from_y(pays[j - 1], -j) for j in (2, 1, 3)]
    self_rows = self_part(node_features, w_self, bias[None, :])
    return finish(own, self_rows, neighbour_count.reshape(SPAN // LANES, LANES), pays)


def solution(mesh):
    return jax.shard_map(
        body,
        mesh=mesh,
        in_specs=(
            P(("row", "col"), None),
            P(("row", "col")),
            P("row", "col", None),
            P("row", "col", None),
            P("row", "col"),
            P("row", "col", None, None, None),
            P(),
            P(),
            P(),
        ),
        out_specs=P(("row", "col"), None),
        check_vma=False,
    )
```
